32 devices in a mesh: row: 4 (over x, core), col: 8 (over z, y).
Axes of the slice: x: 2, y: 2, z: 4, core: 2. Of those that a mesh axis runs over, the one named last changes fastest.
Arguments:
- ancestor_inverse: bfloat16 [32768, 32768], P('row', 'col'), may hold values from -0.03125 to 0.03125
- panel: bfloat16 [32768, 512], P(('row', 'col')), may hold values from -0.75 to 0.75
- structure: int32 [2, 128], replicated, may hold values 0 or 1
- diag_inverse: float32 [2, 256, 256], replicated, may hold values from -6 to 6
Outputs:
- upper: bfloat16 [32768, 512], P(('row', 'col'))
- diagonal: float32 [2, 256, 256], replicated
The draws below stay inside these ranges and needn't reach their ends.
All inputs are finite; a program needn't handle non-finite values.
Results may differ from the reference program's by a relative error of at most 0.0014.
Values may be sent and summed in bfloat16 or wider, within the bound.
No kernel may reach another device: no remote copies, remote signals or barrier semaphores. Data moves between devices by JAX's collectives and lax.ppermute only.
A program may use at most 128 MiB of HBM per device.

```python
import jax
import jax.numpy as jnp
from jax import lax

WIDTH = 256
SNODES = 2
BLOCKS = 128
ROWS = 32768


def touch_ends(entries, key, low, high):
    longest = entries.shape.index(max(entries.shape))
    spots = []
    for shift in (0, 1):
        where = [jax.random.randint(jax.random.fold_in(key, axis), (), 0, length) for axis, length in enumerate(entries.shape)]
        where[longest] = (where[longest] + shift) % entries.shape[longest]
        spots.append(tuple(where))
    return entries.at[spots[0]].set(low).at[spots[1]].set(high)


def level_of(rng, dims, cuts, least, high):
    loudness, own = 1.0, jax.random.fold_in(rng, 6)
    for dim, parts in cuts:
        steps = jnp.exp(jax.random.uniform(jax.random.fold_in(own, dim), (parts,), jnp.float32, least / len(cuts), high / len(cuts)))
        loudness = loudness * jnp.repeat(steps, dims[dim] // parts).reshape([-1 if axis == dim else 1 for axis in range(len(dims))])
    return loudness


def noise(own_key, extent, spread, bound, split=(), held_as=jnp.bfloat16):
    factor_of = level_of(own_key, extent, split, -0.22, 0.18) if split else 1.0
    array = jax.random.normal(own_key, extent, jnp.float32) * spread * factor_of
    return jnp.minimum(jnp.maximum(array, -bound), bound).astype(held_as)


def setup_inputs(seed: int = 0) -> dict:
    key_list = jax.random.split(jax.random.key(seed), 5)
    return {
        "ancestor_inverse": noise(key_list[0], (ROWS, ROWS), ROWS ** -0.5, 0.03125, ((0, 4), (1, 8))),
        "panel": noise(key_list[1], (ROWS, SNODES * WIDTH), 0.125, 0.75, ((0, 32),)),
        "structure": touch_ends((jax.random.randint(key_list[2], (SNODES, BLOCKS), 0, 4) < 3).astype(jnp.int32), jax.random.fold_in(key_list[2], 1), 0, 1),
        "diag_inverse": noise(key_list[3], (SNODES, WIDTH, WIDTH), 1.0, 6.0, (), jnp.float32),
    }


def reference(ancestor_inverse, panel, structure, diag_inverse):
    keeps = jnp.repeat(structure.T.astype(jnp.float32), WIDTH, axis=0)
    keep = jnp.repeat(keeps, WIDTH, axis=1)
    masked = panel * keep.astype(jnp.bfloat16)
    full = -jnp.dot(ancestor_inverse, masked, preferred_element_type=jnp.float32)
    full = full * keep
    upper = full.astype(jnp.bfloat16)
    lower_f = masked.astype(jnp.float32).reshape(ROWS, SNODES, WIDTH)
    upper_f = full.reshape(ROWS, SNODES, WIDTH)
    update = jnp.einsum("mkw,mkv->kwv", lower_f, upper_f, precision=lax.Precision.HIGHEST)
    return upper, diag_inverse - update
```

```python
import functools
import math

import jax
import jax.numpy as jnp
from jax import lax
from jax.experimental import pallas as pl
from jax.experimental.pallas import tpu as pltpu
from jax.sharding import PartitionSpec as P

AXES = ("row", "col")
F32 = jnp.float32
BF16 = jnp.bfloat16
SCALE_ROWS = 16
VMEM_BYTES = 48 * 1024 * 1024


def encode(values, out_ref):
    rows = values.shape[0]
    top = jnp.max(jnp.abs(values), axis=0, keepdims=True)
    power = jnp.floor(14.9 - jnp.log2(jnp.maximum(top, 1e-37)))
    power = jnp.minimum(jnp.maximum(power, -100.0), 120.0)
    coded = jnp.round(values * jnp.exp2(power)).astype(jnp.int32)
    out_ref[0, :rows, :] = coded.astype(jnp.int16)
    powers = jnp.broadcast_to(power, (SCALE_ROWS, values.shape[1]))
    out_ref[0, rows:, :] = powers.astype(jnp.int32).astype(jnp.int16)


def decode(msg_ref):
    rows = msg_ref.shape[1] - SCALE_ROWS
    power = msg_ref[0, rows:, :].astype(jnp.int32).astype(F32)[:1]
    return msg_ref[0, :rows, :].astype(jnp.int32).astype(F32) * jnp.exp2(-power)


def product_kernel(tiles, parts, info_ref, a_ref, *refs):
    b_refs, (msg_ref, own_ref) = refs[:parts], refs[parts:]
    depth = b_refs[0].shape[0]
    total = None
    for part in range(parts):
        start = pl.multiple_of(info_ref[2 + part] * depth, depth)
        term = jnp.dot(a_ref[:, pl.ds(start, depth)], b_refs[part][...], preferred_element_type=F32)
        total = term if total is None else total + term
    step = pl.program_id(0)

    @pl.when(step < tiles)
    def _():
        encode(total, msg_ref)

    @pl.when(step >= tiles)
    def _():
        own_ref[0] = total


def product(info, ancestor, pieces, tile):
    depth, n = pieces[0].shape
    tiles = depth // tile
    parts = len(pieces)
    width = ancestor.shape[1]

    def a_map(i, info_ref):
        piece = jnp.where(i < tiles, info_ref[0], info_ref[1])
        return piece * tiles + lax.rem(i, tiles), 0

    grid_spec = pltpu.PrefetchScalarGridSpec(
        num_scalar_prefetch=1,
        grid=(2 * tiles,),
        in_specs=[pl.BlockSpec((tile, width), a_map)]
        + [pl.BlockSpec((depth, n), lambda i, info_ref: (0, 0))] * parts,
        out_specs=[
            pl.BlockSpec((1, tile + SCALE_ROWS, n), lambda i, info_ref: (jnp.minimum(i, tiles - 1), 0, 0)),
            pl.BlockSpec((1, tile, n), lambda i, info_ref: (jnp.maximum(i - tiles, 0), 0, 0)),
        ],
    )
    return pl.pallas_call(
        functools.partial(product_kernel, tiles, parts),
        grid_spec=grid_spec,
        out_shape=[
            jax.ShapeDtypeStruct((tiles, tile + SCALE_ROWS, n), jnp.int16),
            jax.ShapeDtypeStruct((tiles, tile, n), F32),
        ],
        compiler_params=pltpu.CompilerParams(vmem_limit_bytes=VMEM_BYTES),
        cost_estimate=pl.CostEstimate(
            flops=4 * depth * width * n,
            bytes_accessed=4 * depth * width + 2 * width * n + 6 * depth * n,
            transcendentals=0,
        ),
        name="product",
    )(info, ancestor, *pieces)


def summed(pairs, moved, which):
    total = pairs[0][0][0] + decode(pairs[0][1])
    for place, (own, msg) in enumerate(pairs[1:], 1):
        total = jnp.where(which == place, own[0] + decode(msg), total)
    for msg in moved:
        total = total + decode(msg)
    return total


def pass_on_kernel(count, which_ref, *refs):
    pairs = [(refs[2 * i], refs[2 * i + 1]) for i in range(count)]
    encode(summed(pairs, refs[2 * count : -1], which_ref[0]), refs[-1])


def tile_spec(array):
    return pl.BlockSpec((1,) + array.shape[1:], lambda i, *_: (i, 0, 0))


def pass_on(which, pairs, moved):
    flat = [x for pair in pairs for x in pair] + moved
    msg = pairs[0][1]
    return pl.pallas_call(
        functools.partial(pass_on_kernel, len(pairs)),
        grid_spec=pltpu.PrefetchScalarGridSpec(
            num_scalar_prefetch=1,
            grid=(msg.shape[0],),
            in_specs=[tile_spec(x) for x in flat],
            out_specs=tile_spec(msg),
        ),
        out_shape=jax.ShapeDtypeStruct(msg.shape, msg.dtype),
        compiler_params=pltpu.CompilerParams(vmem_limit_bytes=VMEM_BYTES),
        cost_estimate=pl.CostEstimate(
            flops=8 * msg.size, bytes_accessed=(2 * len(flat) + 6) * msg.size, transcendentals=0
        ),
        name="pass_on",
    )(which, *flat)


def finish_kernel(moved, own_ref, msg_ref, *refs):
    masked_ref, keep_ref, upper_ref, update_ref = refs[moved:]
    total = summed([(own_ref, msg_ref)], refs[:moved], 0)
    full = -total * keep_ref[...].astype(F32)
    upper_ref[...] = full.astype(BF16)
    first = full.astype(BF16)
    rest = full - first.astype(F32)
    second = rest.astype(BF16)
    third = (rest - second.astype(F32)).astype(BF16)
    width = update_ref.shape[1]

    @pl.when(pl.program_id(0) == 0)
    def _():
        update_ref[...] = jnp.zeros_like(update_ref)

    for k in range(update_ref.shape[0]):
        cut = slice(k * width, (k + 1) * width)
        lower = masked_ref[:, cut]
        for part in (third, second, first):
            update_ref[k] += lax.dot_general(
                lower, part[:, cut], (((0,), (0,)), ((), ())), preferred_element_type=F32
            )


def finish(own, msg, moved, masked, keep, width):
    tiles, tile, n = own.shape
    flat = [own, msg] + moved
    plane = pl.BlockSpec((tile, n), lambda i: (i, 0))
    snodes = n // width
    return pl.pallas_call(
        functools.partial(finish_kernel, len(moved)),
        grid=(tiles,),
        in_specs=[tile_spec(x) for x in flat] + [plane, plane],
        out_specs=[plane, pl.BlockSpec((snodes, width, width), lambda i: (0, 0, 0))],
        out_shape=[
            jax.ShapeDtypeStruct((tiles * tile, n), BF16),
            jax.ShapeDtypeStruct((snodes, width, width), F32),
        ],
        compiler_params=pltpu.CompilerParams(vmem_limit_bytes=VMEM_BYTES),
        cost_estimate=pl.CostEstimate(
            flops=6 * own.size * width, bytes_accessed=16 * own.size, transcendentals=0
        ),
        name="finish",
    )(*flat, masked, keep)


def orders(line):
    table = []
    for place in range(line):
        up, down = line - 1 - place, place
        slots = [None] * line
        slots[line - 1] = place
        long, short = (1, -1) if up >= down else (-1, 1)
        for far in range(1, max(up, down) + 1):
            slots[line - 1 - far] = place + long * far
        free = [q for q in range(line) if slots[q] is None]
        for q, far in zip(free, range(min(up, down), 0, -1)):
            slots[q] = place + short * far
        table.append(slots)
    return table


def make_local(rows, cols):
    line = cols // 2
    table = orders(line)

    def at(row, col):
        return row * cols + col

    def swap_low():
        return [(at(r, c), at(r, c ^ 1)) for r in range(rows) for c in range(cols)]

    def along(step):
        return [
            (at(r, c), at(r, c + 2 * step))
            for r in range(rows)
            for c in range(cols)
            if 0 <= c + 2 * step < cols
        ]

    def swap_rows(bit):
        return [(at(r, c), at(r ^ bit, c)) for r in range(rows) for c in range(cols)]

    def swap_line(bit):
        return [(at(r, c), at(r, c ^ (2 * bit))) for r in range(rows) for c in range(cols)]

    def move(array, pairs):
        return lax.ppermute(array, AXES, pairs)

    ratio = cols // rows
    halves = rows // 2

    def gather_pieces(masked, row_index, col_index):
        source = col_index // ratio
        hop = lax.rem(row_index // 2 - source // 2 + halves, halves)
        mine = []
        for group in range(halves):
            got = None
            for g in range(halves):
                pairs = []
                for r in range(rows):
                    for c in range(cols):
                        part = c % rows
                        if part // 2 == group:
                            to_row = (r // 2 + g) % halves * 2 + part % 2
                            pairs.append((at(r, c), at(to_row, r * ratio + c // rows)))
                new = move(masked, pairs)
                got = new if got is None else jnp.where(hop == g, new, got)
            mine.append(got)
        other = [move(x, swap_rows(1)) for x in mine]
        odd = lax.rem(row_index, 2)
        places = [2 * g + odd for g in range(halves)] + [2 * g + 1 - odd for g in range(halves)]
        return mine + other, places

    def gather_whole(masked, row_index, col_index):
        row_block = lax.all_gather(masked, "col", axis=0, tiled=True)
        span = masked.shape[0] * rows
        own = lax.dynamic_slice_in_dim(row_block, lax.rem(col_index, ratio) * span, span, 0)
        own = jnp.where(row_index == col_index // ratio, own, jnp.zeros_like(own))
        block = lax.psum(own, "row")
        pieces = [block[i * masked.shape[0] : (i + 1) * masked.shape[0]] for i in range(rows)]
        return pieces, [jnp.int32(i) for i in range(rows)]

    gather = gather_pieces if halves * halves <= 4 else gather_whole

    def total_update(update, row_index):
        shape = update.shape
        flat = update.reshape(2, -1, shape[-1])
        odd = lax.rem(row_index, 2)
        keep = lax.dynamic_index_in_dim(flat, odd, 0, keepdims=False)
        give = lax.dynamic_index_in_dim(flat, 1 - odd, 0, keepdims=False)
        keep = keep + move(give, swap_rows(1))
        keep = keep + move(keep, swap_low())
        bit = 2
        while bit < rows:
            keep = keep + move(keep, swap_rows(bit))
            bit *= 2
        bit = 1
        while bit < line:
            keep = keep + move(keep, swap_line(bit))
            bit *= 2
        other = move(keep, swap_rows(1))
        even_part = jnp.where(odd == 0, keep, other)
        odd_part = jnp.where(odd == 0, other, keep)
        return jnp.stack([even_part, odd_part]).reshape(shape)

    def local(ancestor_inverse, panel, structure, diag_inverse):
        snodes, width = diag_inverse.shape[:2]
        depth = panel.shape[0]
        tile = min(512, depth)
        row_index, col_index = lax.axis_index("row"), lax.axis_index("col")
        low, place = lax.rem(col_index, 2), col_index // 2
        begin = (row_index * cols + col_index) * depth
        same = math.gcd(depth, width)
        blocks = depth // same
        owners = (begin + jnp.arange(blocks, dtype=jnp.int32) * same) // width
        keep = jnp.take(structure, owners, axis=1).astype(BF16)
        keep = jnp.broadcast_to(keep.T[:, None, :, None], (blocks, same, snodes, width))
        keep = keep.reshape(depth, snodes * width)
        masked = panel * keep
        order = jnp.asarray(table, jnp.int32)[place]
        uppers, updates = [], []
        for k in range(snodes):
            cut = slice(k * width, (k + 1) * width)
            masked_k, keep_k = masked[:, cut], keep[:, cut]
            pieces, places = gather(masked_k, row_index, col_index)
            own, got = [], []
            for q in range(line):
                info = jnp.stack([order[q] * 2 + 1 - low, order[q] * 2 + low] + places)
                msg, kept = product(info, ancestor_inverse, pieces, tile)
                own.append(kept)
                got.append(move(msg, swap_low()))
            moved = {1: None, -1: None}
            for far in range(line - 1, 0, -1):
                for way in (1, -1):
                    senders = [p for p in range(line) if 0 <= p + way * far < line]
                    slot = {p: table[p].index(p + way * far) for p in senders}
                    slots = sorted(set(slot.values()), reverse=True)
                    choice = [slots.index(slot[p]) if p in slot else 0 for p in range(line)]
                    which = jnp.asarray(choice, jnp.int32)[place][None]
                    before = [] if moved[way] is None else [moved[way]]
                    msg = pass_on(which, [(own[q], got[q]) for q in slots], before)
                    moved[way] = move(msg, along(way))
            arrived = [x for x in moved.values() if x is not None]
            upper, update = finish(own[-1], got[-1], arrived, masked_k, keep_k, width)
            uppers.append(upper)
            updates.append(total_update(update, row_index))
        diagonal = diag_inverse - jnp.concatenate(updates)
        return jnp.concatenate(uppers, axis=1), diagonal

    return local


def solution(mesh):
    return jax.shard_map(
        make_local(mesh.shape["row"], mesh.shape["col"]),
        mesh=mesh,
        in_specs=(P("row", "col"), P(("row", "col"), None), P(), P()),
        out_specs=(P(("row", "col"), None), P()),
        check_vma=False,
    )
```

```python
import functools
import math

import jax
import jax.numpy as jnp
from jax import lax
from jax.experimental import pallas as pl
from jax.experimental.pallas import tpu as pltpu
from jax.sharding import PartitionSpec as P

AXES = ("row", "col")
F32 = jnp.float32
BF16 = jnp.bfloat16
SCALE_ROWS = 16
VMEM_BYTES = 16 * 1024 * 1024
LIGHT = pl.CostEstimate(flops=1, bytes_accessed=1, transcendentals=0)
PRODUCT_BYTES = 60 * 1024 * 1024


def encode(values, out_ref):
    rows = values.shape[0]
    top = jnp.max(jnp.abs(values), axis=0, keepdims=True)
    power = jnp.floor(14.9 - jnp.log2(jnp.maximum(top, 1e-37)))
    power = jnp.minimum(jnp.maximum(power, -100.0), 120.0)
    coded = jnp.round(values * jnp.exp2(power)).astype(jnp.int32)
    out_ref[0, :rows, :] = coded.astype(jnp.int16)
    powers = jnp.broadcast_to(power, (SCALE_ROWS, values.shape[1]))
    out_ref[0, rows:, :] = powers.astype(jnp.int32).astype(jnp.int16)


def decode(msg_ref):
    rows = msg_ref.shape[1] - SCALE_ROWS
    power = msg_ref[0, rows:, :].astype(jnp.int32).astype(F32)[:1]
    return msg_ref[0, :rows, :].astype(jnp.int32).astype(F32) * jnp.exp2(-power)


def product_kernel(tiles, parts, info_ref, a_ref, *refs):
    b_refs, outs = refs[:parts], refs[parts:]
    step = pl.program_id(0)
    total = None
    for part, b_ref in enumerate(b_refs):
        size = b_ref.shape[0]
        start = pl.multiple_of(info_ref[2 + part] * size, size)
        term = jnp.dot(a_ref[:, pl.ds(start, size)], b_ref[...], preferred_element_type=F32)
        total = term if total is None else total + term
    n = outs[1].shape[2]
    groups = [total[:, i * n : (i + 1) * n] for i in range(len(outs) // 2)]

    @pl.when(step < tiles)
    def _():
        for group, msg_ref in zip(groups, outs[::2]):
            encode(group, msg_ref)

    @pl.when(step >= tiles)
    def _():
        for group, own_ref in zip(groups, outs[1::2]):
            own_ref[0] = group


def product(info, ancestor, parts, depth, tile, groups):
    n = parts[0].shape[1] // groups
    tiles = depth // tile
    width = ancestor.shape[1]

    def a_map(i, info_ref):
        piece = jnp.where(i < tiles, info_ref[0], info_ref[1])
        return piece * tiles + lax.rem(i, tiles), 0

    msg_spec = pl.BlockSpec((1, tile + SCALE_ROWS, n), lambda i, info_ref: (jnp.minimum(i, tiles - 1), 0, 0))
    own_spec = pl.BlockSpec((1, tile, n), lambda i, info_ref: (jnp.maximum(i - tiles, 0), 0, 0))
    msg_shape = jax.ShapeDtypeStruct((tiles, tile + SCALE_ROWS, n), jnp.int16)
    own_shape = jax.ShapeDtypeStruct((tiles, tile, n), F32)
    outs = pl.pallas_call(
        functools.partial(product_kernel, tiles, len(parts)),
        grid_spec=pltpu.PrefetchScalarGridSpec(
            num_scalar_prefetch=1,
            grid=(2 * tiles,),
            in_specs=[pl.BlockSpec((tile, width), a_map)]
            + [pl.BlockSpec(x.shape, lambda i, info_ref: (0, 0)) for x in parts],
            out_specs=[msg_spec, own_spec] * groups,
        ),
        out_shape=[msg_shape, own_shape] * groups,
        compiler_params=pltpu.CompilerParams(vmem_limit_bytes=PRODUCT_BYTES),
        cost_estimate=LIGHT,
        name="product",
    )(info, ancestor, *parts)
    return outs[::2], outs[1::2]


def summed(pairs, moved, use_ref):
    total = pairs[0][0][0] + decode(pairs[0][1])
    for place, (own, msg) in enumerate(pairs[1:], 1):
        total = jnp.where(use_ref[0] == place, own[0] + decode(msg), total)
    for place, msg in enumerate(moved, 1):
        total = total + jnp.where(use_ref[place] != 0, decode(msg), 0.0)
    return total


def pass_on_kernel(count, use_ref, *refs):
    pairs = [(refs[2 * i], refs[2 * i + 1]) for i in range(count)]
    encode(summed(pairs, refs[2 * count : -1], use_ref), refs[-1])


def tile_spec(array):
    return pl.BlockSpec((1,) + array.shape[1:], lambda i, *_: (i, 0, 0))


def pass_on(use, pairs, moved):
    flat = [x for pair in pairs for x in pair] + moved
    msg = pairs[0][1]
    return pl.pallas_call(
        functools.partial(pass_on_kernel, len(pairs)),
        grid_spec=pltpu.PrefetchScalarGridSpec(
            num_scalar_prefetch=1,
            grid=(msg.shape[0],),
            in_specs=[tile_spec(x) for x in flat],
            out_specs=tile_spec(msg),
        ),
        out_shape=jax.ShapeDtypeStruct(msg.shape, msg.dtype),
        compiler_params=pltpu.CompilerParams(vmem_limit_bytes=VMEM_BYTES),
        cost_estimate=LIGHT,
        name="pass_on",
    )(use, *flat)


def finish_kernel(moved, use_ref, own_ref, msg_ref, *refs):
    masked_ref, keep_ref, upper_ref, update_ref = refs[moved:]
    total = summed([(own_ref, msg_ref)], refs[:moved], use_ref)
    full = -total * keep_ref[...].astype(F32)
    upper_ref[...] = full.astype(BF16)
    first = full.astype(BF16)
    rest = full - first.astype(F32)
    second = rest.astype(BF16)
    third = (rest - second.astype(F32)).astype(BF16)
    width = update_ref.shape[1]

    @pl.when(pl.program_id(0) == 0)
    def _():
        update_ref[...] = jnp.zeros_like(update_ref)

    for k in range(update_ref.shape[0]):
        cut = slice(k * width, (k + 1) * width)
        lower = masked_ref[:, cut]
        for part in (third, second, first):
            update_ref[k] += lax.dot_general(
                lower, part[:, cut], (((0,), (0,)), ((), ())), preferred_element_type=F32
            )


def finish(use, own, msg, moved, masked, keep, width):
    tiles, tile, n = own.shape
    flat = [own, msg] + moved
    plane = pl.BlockSpec((tile, n), lambda i, use_ref: (i, 0))
    snodes = n // width
    return pl.pallas_call(
        functools.partial(finish_kernel, len(moved)),
        grid_spec=pltpu.PrefetchScalarGridSpec(
            num_scalar_prefetch=1,
            grid=(tiles,),
            in_specs=[tile_spec(x) for x in flat] + [plane, plane],
            out_specs=[plane, pl.BlockSpec((snodes, width, width), lambda i, use_ref: (0, 0, 0))],
        ),
        out_shape=[
            jax.ShapeDtypeStruct((tiles * tile, n), BF16),
            jax.ShapeDtypeStruct((snodes, width, width), F32),
        ],
        compiler_params=pltpu.CompilerParams(vmem_limit_bytes=VMEM_BYTES),
        cost_estimate=LIGHT,
        name="finish",
    )(use, *flat, masked, keep)


def line_rounds(line):
    pending = {}
    for place in range(line):
        pending[place, 1] = list(range(line - 1, place, -1))
        pending[place, -1] = list(range(place))
    arrived = set()
    rounds = []
    while any(pending.values()):
        sends = {}
        for place in range(line):
            way = 1 if (place + len(rounds)) % 2 == 0 else -1
            behind = 0 <= place - way < line
            for part in pending[place, way]:
                if not behind or (place, part) in arrived:
                    sends[place] = (part, place + way)
                    break
        for place, (part, to) in sends.items():
            pending[place, to - place].remove(part)
        arrived |= {(to, part) for part, to in sends.values() if part != to}
        rounds.append(sends)
    return rounds


def orders(line, rounds):
    return [[sends[place][0] for sends in rounds if place in sends] + [place] for place in range(line)]


def make_local(rows, cols):
    line = cols // 2
    rounds = line_rounds(line)
    table = orders(line, rounds)

    def at(row, col):
        return row * cols + col

    def swap_low():
        return [(at(r, c), at(r, c ^ 1)) for r in range(rows) for c in range(cols)]

    def along(sends):
        return [
            (at(r, 2 * place + low), at(r, 2 * to + low))
            for r in range(rows)
            for place, (_, to) in sends.items()
            for low in range(2)
        ]

    def needs(turn):
        sends = rounds[turn] if turn < len(rounds) else {p: (p, p) for p in range(line)}
        slot = {p: table[p].index(part) for p, (part, _) in sends.items()}
        slots = sorted(set(slot.values()))
        choice = [slots.index(slot[p]) if p in slot else 0 for p in range(line)]
        used = {}
        for before in range(turn):
            for part, to in rounds[before].values():
                if to in sends and sends[to][0] == part:
                    used.setdefault(before, set()).add(to)
        flags = [[int(p in places) for p in range(line)] for places in used.values()]
        return slots, list(used), list(zip(choice, *flags))

    def swap_rows(bit):
        return [(at(r, c), at(r ^ bit, c)) for r in range(rows) for c in range(cols)]

    def swap_line(bit):
        return [(at(r, c), at(r, c ^ (2 * bit))) for r in range(rows) for c in range(cols)]

    def move(array, pairs):
        return lax.ppermute(array, AXES, pairs)

    ratio = cols // rows

    def gather_pieces(masked, row_index, col_index):
        half = masked.shape[0] // 2
        plane, odd = row_index // 2, lax.rem(row_index, 2)
        stay = lax.dynamic_slice_in_dim(masked, plane * half, half, 0)
        cross = lax.dynamic_slice_in_dim(masked, (1 - plane) * half, half, 0)
        cross = move(cross, swap_rows(2))
        is_own = col_index // ratio // 2 == plane
        upper_half = lax.rem(col_index, rows) // 2
        parts, places = [], []
        for turn in (0, 1):
            pairs = []
            for r in range(rows):
                for c in range(cols):
                    flip = 0 if c % rows // 2 == turn else 2
                    pairs.append((at(r, c), at(r // 2 * 2 + c % 2, (r ^ flip) * ratio + c // rows)))
            mine = move(jnp.where(upper_half == turn, stay, cross), pairs)
            other = move(mine, swap_rows(2))
            pair = jnp.where(is_own, turn, 1 - turn)
            parts += [mine, other, move(mine, swap_rows(1)), move(other, swap_rows(1))]
            for side in (odd, 1 - odd):
                places += [2 * (2 * pair + side) + plane, 2 * (2 * (1 - pair) + side) + 1 - plane]
        return parts, places

    def gather_whole(masked, row_index, col_index):
        row_block = lax.all_gather(masked, "col", axis=0, tiled=True)
        span = masked.shape[0] * rows
        own = lax.dynamic_slice_in_dim(row_block, lax.rem(col_index, ratio) * span, span, 0)
        own = jnp.where(row_index == col_index // ratio, own, jnp.zeros_like(own))
        block = lax.psum(own, "row")
        pieces = [block[i * masked.shape[0] : (i + 1) * masked.shape[0]] for i in range(rows)]
        return pieces, [jnp.int32(i) for i in range(rows)]

    gather = gather_pieces if rows == 4 else gather_whole

    def total_update(update, row_index):
        shape = update.shape
        flat = update.reshape(2, -1, shape[-1])
        odd = lax.rem(row_index, 2)
        keep = lax.dynamic_index_in_dim(flat, odd, 0, keepdims=False)
        give = lax.dynamic_index_in_dim(flat, 1 - odd, 0, keepdims=False)
        keep = keep + move(give, swap_rows(1))
        keep = keep + move(keep, swap_low())
        bit = 2
        while bit < rows:
            keep = keep + move(keep, swap_rows(bit))
            bit *= 2
        bit = 1
        while bit < line:
            keep = keep + move(keep, swap_line(bit))
            bit *= 2
        other = move(keep, swap_rows(1))
        even_part = jnp.where(odd == 0, keep, other)
        odd_part = jnp.where(odd == 0, other, keep)
        return jnp.stack([even_part, odd_part]).reshape(shape)

    def local(ancestor_inverse, panel, structure, diag_inverse):
        snodes, width = diag_inverse.shape[:2]
        depth = panel.shape[0]
        tile = min(512, depth)
        row_index, col_index = lax.axis_index("row"), lax.axis_index("col")
        low, place = lax.rem(col_index, 2), col_index // 2
        begin = (row_index * cols + col_index) * depth
        same = math.gcd(depth, width)
        blocks = depth // same
        owners = (begin + jnp.arange(blocks, dtype=jnp.int32) * same) // width
        keep = jnp.take(structure, owners, axis=1).astype(BF16)
        keep = jnp.broadcast_to(keep.T[:, None, :, None], (blocks, same, snodes, width))
        keep = keep.reshape(depth, snodes * width)
        masked = panel * keep
        order = jnp.asarray(table, jnp.int32)[place]
        cuts = [slice(k * width, (k + 1) * width) for k in range(snodes)]
        pieces, places = gather(masked, row_index, col_index)
        own = [[None] * line for _ in cuts]
        got = [[None] * line for _ in cuts]
        moved = [[] for _ in cuts]
        last = order

        def multiply(q):
            nonlocal last
            info = jnp.stack([order[q] * 2 + 1 - low, order[q] * 2 + low] + places)
            info, last = lax.optimization_barrier((info, last))
            msgs, kept = product(info, ancestor_inverse, pieces, depth, tile, snodes)
            for k in range(snodes):
                own[k][q] = kept[k]
                got[k][q] = move(msgs[k], swap_low())
            last = msgs[-1]

        def advance(turn, k):
            nonlocal last
            slots, before, use = needs(turn)
            use, last = lax.optimization_barrier((jnp.asarray(use, jnp.int32)[place], last))
            last = pass_on(use, [(own[k][q], got[k][q]) for q in slots], [moved[k][t] for t in before])
            moved[k].append(move(last, along(rounds[turn])))

        multiply(0)
        ready = 1
        for turn in range(len(rounds)):
            while ready < line and ready <= max(needs(turn)[0]) + (turn != 1):
                multiply(ready)
                ready += 1
            for k in range(snodes):
                advance(turn, k)
        while ready < line:
            multiply(ready)
            ready += 1
        _, before, use = needs(len(rounds))
        use = jnp.asarray(use, jnp.int32)[place]
        uppers, updates = [], []
        for k, cut in enumerate(cuts):
            arrived = [moved[k][t] for t in before]
            upper, update = finish(
                use, own[k][-1], got[k][-1], arrived, masked[:, cut], keep[:, cut], width
            )
            uppers.append(upper)
            updates.append(total_update(update, row_index))
        return jnp.concatenate(uppers, axis=1), diag_inverse - jnp.concatenate(updates)

    return local


def solution(mesh):
    return jax.shard_map(
        make_local(mesh.shape["row"], mesh.shape["col"]),
        mesh=mesh,
        in_specs=(P("row", "col"), P(("row", "col"), None), P(), P()),
        out_specs=(P(("row", "col"), None), P()),
        check_vma=False,
    )
```

```python
import functools
import math

import jax
import jax.numpy as jnp
from jax import lax
from jax.experimental import pallas as pl
from jax.experimental.pallas import tpu as pltpu
from jax.sharding import PartitionSpec as P

AXES = ("row", "col")
F32 = jnp.float32
BF16 = jnp.bfloat16
SCALE_ROWS = 16
VMEM_BYTES = 16 * 1024 * 1024


def cost(flops, size):
    return pl.CostEstimate(flops=int(flops), bytes_accessed=int(size), transcendentals=0)


PRODUCT_BYTES = 36 * 1024 * 1024


def encode(values, out_ref):
    rows = values.shape[0]
    top = jnp.max(jnp.abs(values), axis=0, keepdims=True)
    power = jnp.floor(14.9 - jnp.log2(jnp.maximum(top, 1e-37)))
    power = jnp.minimum(jnp.maximum(power, -100.0), 120.0)
    coded = jnp.round(values * jnp.exp2(power)).astype(jnp.int32)
    out_ref[0, :rows, :] = coded.astype(jnp.int16)
    powers = jnp.broadcast_to(power, (SCALE_ROWS, values.shape[1]))
    out_ref[0, rows:, :] = powers.astype(jnp.int32).astype(jnp.int16)


def decode(msg_ref):
    rows = msg_ref.shape[1] - SCALE_ROWS
    power = msg_ref[0, rows:, :].astype(jnp.int32).astype(F32)[:1]
    return msg_ref[0, :rows, :].astype(jnp.int32).astype(F32) * jnp.exp2(-power)


def product_kernel(tiles, parts, info_ref, a_ref, *refs):
    b_refs, outs = refs[:parts], refs[parts:]
    step = pl.program_id(0)
    total = None
    for part, b_ref in enumerate(b_refs):
        size = b_ref.shape[0]
        start = pl.multiple_of(info_ref[2 + part] * size, size)
        term = jnp.dot(a_ref[:, pl.ds(start, size)], b_ref[...], preferred_element_type=F32)
        total = term if total is None else total + term
    n = outs[1].shape[2]
    groups = [total[:, i * n : (i + 1) * n] for i in range(len(outs) // 2)]

    @pl.when(step < tiles)
    def _():
        for group, msg_ref in zip(groups, outs[::2]):
            encode(group, msg_ref)

    @pl.when(step >= tiles)
    def _():
        for group, own_ref in zip(groups, outs[1::2]):
            own_ref[0] = group


def product(info, ancestor, parts, depth, tile, groups):
    n = parts[0].shape[1] // groups
    tiles = depth // tile
    width = ancestor.shape[1]

    def a_map(i, info_ref):
        piece = jnp.where(i < tiles, info_ref[0], info_ref[1])
        return piece * tiles + lax.rem(i, tiles), 0

    msg_spec = pl.BlockSpec((1, tile + SCALE_ROWS, n), lambda i, info_ref: (jnp.minimum(i, tiles - 1), 0, 0))
    own_spec = pl.BlockSpec((1, tile, n), lambda i, info_ref: (jnp.maximum(i - tiles, 0), 0, 0))
    msg_shape = jax.ShapeDtypeStruct((tiles, tile + SCALE_ROWS, n), jnp.int16)
    own_shape = jax.ShapeDtypeStruct((tiles, tile, n), F32)
    outs = pl.pallas_call(
        functools.partial(product_kernel, tiles, len(parts)),
        grid_spec=pltpu.PrefetchScalarGridSpec(
            num_scalar_prefetch=1,
            grid=(2 * tiles,),
            in_specs=[pl.BlockSpec((tile, width), a_map)]
            + [pl.BlockSpec(x.shape, lambda i, info_ref: (0, 0)) for x in parts],
            out_specs=[msg_spec, own_spec] * groups,
        ),
        out_shape=[msg_shape, own_shape] * groups,
        compiler_params=pltpu.CompilerParams(vmem_limit_bytes=PRODUCT_BYTES),
        cost_estimate=cost(4 * depth * width * n * groups, 4 * depth * width),
        name="product",
    )(info, ancestor, *parts)
    return outs[::2], outs[1::2]


def summed(pairs, moved, use_ref):
    total = pairs[0][0][0] + decode(pairs[0][1])
    for place, (own, msg) in enumerate(pairs[1:], 1):
        total = jnp.where(use_ref[0] == place, own[0] + decode(msg), total)
    for place, msg in enumerate(moved, 1):
        total = total + jnp.where(use_ref[place] != 0, decode(msg), 0.0)
    return total


def pass_on_kernel(count, use_ref, *refs):
    pairs = [(refs[2 * i], refs[2 * i + 1]) for i in range(count)]
    encode(summed(pairs, refs[2 * count : -1], use_ref), refs[-1])


def tile_spec(array):
    return pl.BlockSpec((1,) + array.shape[1:], lambda i, *_: (i, 0, 0))


def pass_on(use, pairs, moved):
    flat = [x for pair in pairs for x in pair] + moved
    msg = pairs[0][1]
    return pl.pallas_call(
        functools.partial(pass_on_kernel, len(pairs)),
        grid_spec=pltpu.PrefetchScalarGridSpec(
            num_scalar_prefetch=1,
            grid=(msg.shape[0],),
            in_specs=[tile_spec(x) for x in flat],
            out_specs=tile_spec(msg),
        ),
        out_shape=jax.ShapeDtypeStruct(msg.shape, msg.dtype),
        compiler_params=pltpu.CompilerParams(vmem_limit_bytes=VMEM_BYTES),
        cost_estimate=cost(0, 8 * msg.size),
        name="pass_on",
    )(use, *flat)


def finish_kernel(moved, use_ref, own_ref, msg_ref, *refs):
    masked_ref, keep_ref, upper_ref, update_ref = refs[moved:]
    total = summed([(own_ref, msg_ref)], refs[:moved], use_ref)
    full = -total * keep_ref[...].astype(F32)
    upper_ref[...] = full.astype(BF16)
    first = full.astype(BF16)
    rest = full - first.astype(F32)
    second = rest.astype(BF16)
    third = (rest - second.astype(F32)).astype(BF16)
    width = update_ref.shape[1]

    @pl.when(pl.program_id(0) == 0)
    def _():
        update_ref[...] = jnp.zeros_like(update_ref)

    for k in range(update_ref.shape[0]):
        cut = slice(k * width, (k + 1) * width)
        lower = masked_ref[:, cut]
        for part in (third, second, first):
            update_ref[k] += lax.dot_general(
                lower, part[:, cut], (((0,), (0,)), ((), ())), preferred_element_type=F32
            )


def finish(use, own, msg, moved, masked, keep, width):
    tiles, tile, n = own.shape
    flat = [own, msg] + moved
    plane = pl.BlockSpec((tile, n), lambda i, use_ref: (i, 0))
    snodes = n // width
    return pl.pallas_call(
        functools.partial(finish_kernel, len(moved)),
        grid_spec=pltpu.PrefetchScalarGridSpec(
            num_scalar_prefetch=1,
            grid=(tiles,),
            in_specs=[tile_spec(x) for x in flat] + [plane, plane],
            out_specs=[plane, pl.BlockSpec((snodes, width, width), lambda i, use_ref: (0, 0, 0))],
        ),
        out_shape=[
            jax.ShapeDtypeStruct((tiles * tile, n), BF16),
            jax.ShapeDtypeStruct((snodes, width, width), F32),
        ],
        compiler_params=pltpu.CompilerParams(vmem_limit_bytes=VMEM_BYTES),
        cost_estimate=cost(0, 12 * masked.size),
        name="finish",
    )(use, *flat, masked, keep)


def line_rounds(line):
    pending = {}
    for place in range(line):
        pending[place, 1] = list(range(line - 1, place, -1))
        pending[place, -1] = list(range(place))
    arrived = set()
    rounds = []
    while any(pending.values()):
        sends = {}
        for place in range(line):
            way = 1 if (place + len(rounds)) % 2 == 0 else -1
            behind = 0 <= place - way < line
            for part in pending[place, way]:
                if not behind or (place, part) in arrived:
                    sends[place] = (part, place + way)
                    break
        for place, (part, to) in sends.items():
            pending[place, to - place].remove(part)
        arrived |= {(to, part) for part, to in sends.values() if part != to}
        rounds.append(sends)
    return rounds


def orders(line, rounds):
    return [[sends[place][0] for sends in rounds if place in sends] + [place] for place in range(line)]


def make_local(rows, cols):
    line = cols // 2
    rounds = line_rounds(line)
    table = orders(line, rounds)

    def at(row, col):
        return row * cols + col

    def swap_low():
        return [(at(r, c), at(r, c ^ 1)) for r in range(rows) for c in range(cols)]

    def along(sends):
        return [
            (at(r, 2 * place + low), at(r, 2 * to + low))
            for r in range(rows)
            for place, (_, to) in sends.items()
            for low in range(2)
        ]

    def needs(turn):
        sends = rounds[turn] if turn < len(rounds) else {p: (p, p) for p in range(line)}
        slot = {p: table[p].index(part) for p, (part, _) in sends.items()}
        slots = sorted(set(slot.values()))
        choice = [slots.index(slot[p]) if p in slot else 0 for p in range(line)]
        used = {}
        for before in range(turn):
            for part, to in rounds[before].values():
                if to in sends and sends[to][0] == part:
                    used.setdefault(before, set()).add(to)
        flags = [[int(p in places) for p in range(line)] for places in used.values()]
        return slots, list(used), list(zip(choice, *flags))

    def swap_rows(bit):
        return [(at(r, c), at(r ^ bit, c)) for r in range(rows) for c in range(cols)]

    def swap_line(bit):
        return [(at(r, c), at(r, c ^ (2 * bit))) for r in range(rows) for c in range(cols)]

    def move(array, pairs):
        return lax.ppermute(array, AXES, pairs)

    ratio = cols // rows

    def gather_pieces(masked, row_index, col_index):
        half = masked.shape[0] // 2
        plane, odd = row_index // 2, lax.rem(row_index, 2)
        stay = lax.dynamic_slice_in_dim(masked, plane * half, half, 0)
        cross = lax.dynamic_slice_in_dim(masked, (1 - plane) * half, half, 0)
        cross = move(cross, swap_rows(2))
        is_own = col_index // ratio // 2 == plane
        upper_half = lax.rem(col_index, rows) // 2
        parts, places = [], []
        for turn in (0, 1):
            pairs = []
            for r in range(rows):
                for c in range(cols):
                    flip = 0 if c % rows // 2 == turn else 2
                    pairs.append((at(r, c), at(r // 2 * 2 + c % 2, (r ^ flip) * ratio + c // rows)))
            mine = move(jnp.where(upper_half == turn, stay, cross), pairs)
            other = move(mine, swap_rows(2))
            pair = jnp.where(is_own, turn, 1 - turn)
            parts += [mine, other, move(mine, swap_rows(1)), move(other, swap_rows(1))]
            for side in (odd, 1 - odd):
                places += [2 * (2 * pair + side) + plane, 2 * (2 * (1 - pair) + side) + 1 - plane]
        return parts, places

    def gather_whole(masked, row_index, col_index):
        row_block = lax.all_gather(masked, "col", axis=0, tiled=True)
        span = masked.shape[0] * rows
        own = lax.dynamic_slice_in_dim(row_block, lax.rem(col_index, ratio) * span, span, 0)
        own = jnp.where(row_index == col_index // ratio, own, jnp.zeros_like(own))
        block = lax.psum(own, "row")
        pieces = [block[i * masked.shape[0] : (i + 1) * masked.shape[0]] for i in range(rows)]
        return pieces, [jnp.int32(i) for i in range(rows)]

    gather = gather_pieces if rows == 4 else gather_whole

    def total_update(update, row_index):
        shape = update.shape
        flat = update.reshape(2, -1, shape[-1])
        odd = lax.rem(row_index, 2)
        keep = lax.dynamic_index_in_dim(flat, odd, 0, keepdims=False)
        give = lax.dynamic_index_in_dim(flat, 1 - odd, 0, keepdims=False)
        keep = keep + move(give, swap_rows(1))
        keep = keep + move(keep, swap_low())
        bit = 2
        while bit < rows:
            keep = keep + move(keep, swap_rows(bit))
            bit *= 2
        bit = 1
        while bit < line:
            keep = keep + move(keep, swap_line(bit))
            bit *= 2
        other = move(keep, swap_rows(1))
        even_part = jnp.where(odd == 0, keep, other)
        odd_part = jnp.where(odd == 0, other, keep)
        return jnp.stack([even_part, odd_part]).reshape(shape)

    def local(ancestor_inverse, panel, structure, diag_inverse):
        snodes, width = diag_inverse.shape[:2]
        depth = panel.shape[0]
        tile = min(512, depth)
        row_index, col_index = lax.axis_index("row"), lax.axis_index("col")
        low, place = lax.rem(col_index, 2), col_index // 2
        begin = (row_index * cols + col_index) * depth
        same = math.gcd(depth, width)
        blocks = depth // same
        owners = (begin + jnp.arange(blocks, dtype=jnp.int32) * same) // width
        keep = jnp.take(structure, owners, axis=1).astype(BF16)
        keep = jnp.broadcast_to(keep.T[:, None, :, None], (blocks, same, snodes, width))
        keep = keep.reshape(depth, snodes * width)
        masked = panel * keep
        order = jnp.asarray(table, jnp.int32)[place]
        cuts = [slice(k * width, (k + 1) * width) for k in range(snodes)]
        pieces, places = gather(masked, row_index, col_index)
        own = [[None] * line for _ in cuts]
        got = [[None] * line for _ in cuts]
        moved = [[] for _ in cuts]
        last = order

        def multiply(q):
            nonlocal last
            info = jnp.stack([order[q] * 2 + 1 - low, order[q] * 2 + low] + places)
            msgs, kept = product(info, ancestor_inverse, pieces, depth, tile, snodes)
            for k in range(snodes):
                own[k][q] = kept[k]
                got[k][q] = move(msgs[k], swap_low())
            last = msgs[-1]

        def advance(turn, k):
            slots, before, use = needs(turn)
            use = jnp.asarray(use, jnp.int32)[place]
            sent = pass_on(use, [(own[k][q], got[k][q]) for q in slots], [moved[k][t] for t in before])
            moved[k].append(move(sent, along(rounds[turn])))

        multiply(0)
        ready = 1
        for turn in range(len(rounds)):
            while ready < line and ready <= max(needs(turn)[0]) + (turn != 1):
                multiply(ready)
                ready += 1
            for k in range(snodes):
                advance(turn, k)
        while ready < line:
            multiply(ready)
            ready += 1
        _, before, use = needs(len(rounds))
        use = jnp.asarray(use, jnp.int32)[place]
        uppers, updates = [], []
        for k, cut in enumerate(cuts):
            arrived = [moved[k][t] for t in before]
            upper, update = finish(
                use, own[k][-1], got[k][-1], arrived, masked[:, cut], keep[:, cut], width
            )
            uppers.append(upper)
            updates.append(total_update(update, row_index))
        return jnp.concatenate(uppers, axis=1), diag_inverse - jnp.concatenate(updates)

    return local


def solution(mesh):
    return jax.shard_map(
        make_local(mesh.shape["row"], mesh.shape["col"]),
        mesh=mesh,
        in_specs=(P("row", "col"), P(("row", "col"), None), P(), P()),
        out_specs=(P(("row", "col"), None), P()),
        check_vma=False,
    )
```

```python
import functools
import math

import jax
import jax.numpy as jnp
from jax import lax
from jax.experimental import pallas as pl
from jax.experimental.pallas import tpu as pltpu
from jax.sharding import PartitionSpec as P

AXES = ("row", "col")
F32 = jnp.float32
BF16 = jnp.bfloat16
SCALE_ROWS = 16
VMEM_BYTES = 16 * 1024 * 1024


def cost(flops, size):
    return pl.CostEstimate(flops=int(flops), bytes_accessed=int(size), transcendentals=0)


PRODUCT_BYTES = 32 * 1024 * 1024


def encode(values, out_ref):
    rows = values.shape[0]
    top = jnp.max(jnp.abs(values), axis=0, keepdims=True)
    power = jnp.floor(14.9 - jnp.log2(jnp.maximum(top, 1e-37)))
    power = jnp.minimum(jnp.maximum(power, -100.0), 120.0)
    coded = jnp.round(values * jnp.exp2(power)).astype(jnp.int32)
    out_ref[0, :rows, :] = coded.astype(jnp.int16)
    powers = jnp.broadcast_to(power, (SCALE_ROWS, values.shape[1]))
    out_ref[0, rows:, :] = powers.astype(jnp.int32).astype(jnp.int16)


def decode(msg_ref):
    rows = msg_ref.shape[1] - SCALE_ROWS
    power = msg_ref[0, rows:, :].astype(jnp.int32).astype(F32)[:1]
    return msg_ref[0, :rows, :].astype(jnp.int32).astype(F32) * jnp.exp2(-power)


def product_kernel(tiles, parts, info_ref, a_ref, *refs):
    b_refs, outs = refs[:parts], refs[parts:]
    step = pl.program_id(0)
    total = None
    for part, b_ref in enumerate(b_refs):
        size = b_ref.shape[0]
        start = pl.multiple_of(info_ref[2 + part] * size, size)
        term = jnp.dot(a_ref[:, pl.ds(start, size)], b_ref[...], preferred_element_type=F32)
        total = term if total is None else total + term
    n = outs[1].shape[2]
    groups = [total[:, i * n : (i + 1) * n] for i in range(len(outs) // 2)]

    @pl.when(step < tiles)
    def _():
        for group, msg_ref in zip(groups, outs[::2]):
            encode(group, msg_ref)

    @pl.when(step >= tiles)
    def _():
        for group, own_ref in zip(groups, outs[1::2]):
            own_ref[0] = group


def product(info, ancestor, parts, depth, tile, groups):
    n = parts[0].shape[1] // groups
    tiles = depth // tile
    width = ancestor.shape[1]

    def a_map(i, info_ref):
        piece = jnp.where(i < tiles, info_ref[0], info_ref[1])
        return piece * tiles + lax.rem(i, tiles), 0

    msg_spec = pl.BlockSpec((1, tile + SCALE_ROWS, n), lambda i, info_ref: (jnp.minimum(i, tiles - 1), 0, 0))
    own_spec = pl.BlockSpec((1, tile, n), lambda i, info_ref: (jnp.maximum(i - tiles, 0), 0, 0))
    msg_shape = jax.ShapeDtypeStruct((tiles, tile + SCALE_ROWS, n), jnp.int16)
    own_shape = jax.ShapeDtypeStruct((tiles, tile, n), F32)
    outs = pl.pallas_call(
        functools.partial(product_kernel, tiles, len(parts)),
        grid_spec=pltpu.PrefetchScalarGridSpec(
            num_scalar_prefetch=1,
            grid=(2 * tiles,),
            in_specs=[pl.BlockSpec((tile, width), a_map)]
            + [pl.BlockSpec(x.shape, lambda i, info_ref: (0, 0), pipeline_mode=pl.Buffered(1)) for x in parts],
            out_specs=[msg_spec, own_spec] * groups,
        ),
        out_shape=[msg_shape, own_shape] * groups,
        compiler_params=pltpu.CompilerParams(vmem_limit_bytes=PRODUCT_BYTES),
        cost_estimate=cost(4 * depth * width * n * groups, 4 * depth * width),
        name="product",
    )(info, ancestor, *parts)
    return outs[::2], outs[1::2]


def summed(pairs, moved, use_ref):
    total = pairs[0][0][0] + decode(pairs[0][1])
    for place, (own, msg) in enumerate(pairs[1:], 1):
        total = jnp.where(use_ref[0] == place, own[0] + decode(msg), total)
    for place, msg in enumerate(moved, 1):
        total = total + jnp.where(use_ref[place] != 0, decode(msg), 0.0)
    return total


def pass_on_kernel(count, use_ref, *refs):
    pairs = [(refs[2 * i], refs[2 * i + 1]) for i in range(count)]
    encode(summed(pairs, refs[2 * count : -1], use_ref), refs[-1])


def tile_spec(array):
    return pl.BlockSpec((1,) + array.shape[1:], lambda i, *_: (i, 0, 0))


def pass_on(use, pairs, moved):
    flat = [x for pair in pairs for x in pair] + moved
    msg = pairs[0][1]
    return pl.pallas_call(
        functools.partial(pass_on_kernel, len(pairs)),
        grid_spec=pltpu.PrefetchScalarGridSpec(
            num_scalar_prefetch=1,
            grid=(msg.shape[0],),
            in_specs=[tile_spec(x) for x in flat],
            out_specs=tile_spec(msg),
        ),
        out_shape=jax.ShapeDtypeStruct(msg.shape, msg.dtype),
        compiler_params=pltpu.CompilerParams(vmem_limit_bytes=VMEM_BYTES),
        cost_estimate=cost(0, 8 * msg.size),
        name="pass_on",
    )(use, *flat)


def finish_kernel(moved, use_ref, own_ref, msg_ref, *refs):
    masked_ref, keep_ref, upper_ref, update_ref = refs[moved:]
    total = summed([(own_ref, msg_ref)], refs[:moved], use_ref)
    full = -total * keep_ref[...].astype(F32)
    upper_ref[...] = full.astype(BF16)
    first = full.astype(BF16)
    rest = full - first.astype(F32)
    second = rest.astype(BF16)
    third = (rest - second.astype(F32)).astype(BF16)
    width = update_ref.shape[1]

    @pl.when(pl.program_id(0) == 0)
    def _():
        update_ref[...] = jnp.zeros_like(update_ref)

    for k in range(update_ref.shape[0]):
        cut = slice(k * width, (k + 1) * width)
        lower = masked_ref[:, cut]
        for part in (third, second, first):
            update_ref[k] += lax.dot_general(
                lower, part[:, cut], (((0,), (0,)), ((), ())), preferred_element_type=F32
            )


def finish(use, own, msg, moved, masked, keep, width):
    tiles, tile, n = own.shape
    flat = [own, msg] + moved
    plane = pl.BlockSpec((tile, n), lambda i, use_ref: (i, 0))
    snodes = n // width
    return pl.pallas_call(
        functools.partial(finish_kernel, len(moved)),
        grid_spec=pltpu.PrefetchScalarGridSpec(
            num_scalar_prefetch=1,
            grid=(tiles,),
            in_specs=[tile_spec(x) for x in flat] + [plane, plane],
            out_specs=[plane, pl.BlockSpec((snodes, width, width), lambda i, use_ref: (0, 0, 0))],
        ),
        out_shape=[
            jax.ShapeDtypeStruct((tiles * tile, n), BF16),
            jax.ShapeDtypeStruct((snodes, width, width), F32),
        ],
        compiler_params=pltpu.CompilerParams(vmem_limit_bytes=VMEM_BYTES),
        cost_estimate=cost(0, 12 * masked.size),
        name="finish",
    )(use, *flat, masked, keep)


def line_rounds(line):
    pending = {}
    for place in range(line):
        pending[place, 1] = list(range(line - 1, place, -1))
        pending[place, -1] = list(range(place))
    arrived = set()
    rounds = []
    while any(pending.values()):
        sends = {}
        for place in range(line):
            way = 1 if (place + len(rounds)) % 2 == 0 else -1
            behind = 0 <= place - way < line
            for part in pending[place, way]:
                if not behind or (place, part) in arrived:
                    sends[place] = (part, place + way)
                    break
        for place, (part, to) in sends.items():
            pending[place, to - place].remove(part)
        arrived |= {(to, part) for part, to in sends.values() if part != to}
        rounds.append(sends)
    return rounds


def orders(line, rounds):
    return [[sends[place][0] for sends in rounds if place in sends] + [place] for place in range(line)]


def make_local(rows, cols):
    line = cols // 2
    rounds = line_rounds(line)
    table = orders(line, rounds)

    def at(row, col):
        return row * cols + col

    def swap_low():
        return [(at(r, c), at(r, c ^ 1)) for r in range(rows) for c in range(cols)]

    def along(sends):
        return [
            (at(r, 2 * place + low), at(r, 2 * to + low))
            for r in range(rows)
            for place, (_, to) in sends.items()
            for low in range(2)
        ]

    def needs(turn):
        sends = rounds[turn] if turn < len(rounds) else {p: (p, p) for p in range(line)}
        slot = {p: table[p].index(part) for p, (part, _) in sends.items()}
        slots = sorted(set(slot.values()))
        choice = [slots.index(slot[p]) if p in slot else 0 for p in range(line)]
        used = {}
        for before in range(turn):
            for part, to in rounds[before].values():
                if to in sends and sends[to][0] == part:
                    used.setdefault(before, set()).add(to)
        flags = [[int(p in places) for p in range(line)] for places in used.values()]
        return slots, list(used), list(zip(choice, *flags))

    def swap_rows(bit):
        return [(at(r, c), at(r ^ bit, c)) for r in range(rows) for c in range(cols)]

    def swap_line(bit):
        return [(at(r, c), at(r, c ^ (2 * bit))) for r in range(rows) for c in range(cols)]

    def move(array, pairs):
        return lax.ppermute(array, AXES, pairs)

    ratio = cols // rows

    def gather_pieces(masked, row_index, col_index, panel, keep_of):
        half = masked.shape[0] // 2
        plane, odd = row_index // 2, lax.rem(row_index, 2)
        stay = lax.dynamic_slice_in_dim(masked, plane * half, half, 0)
        cross = lax.dynamic_slice_in_dim(panel, (1 - plane) * half, half, 0)
        begin = ((row_index + 2 - 4 * lax.rem(plane, 2)) * cols + col_index) * 2 * half + plane * half
        cross = move(cross, swap_rows(2)) * keep_of(begin, half)
        is_own = col_index // ratio // 2 == plane
        upper_half = lax.rem(col_index, rows) // 2
        parts, places = [], []
        for turn in (0, 1):
            pairs = []
            for r in range(rows):
                for c in range(cols):
                    flip = 0 if c % rows // 2 == turn else 2
                    pairs.append((at(r, c), at(r // 2 * 2 + c % 2, (r ^ flip) * ratio + c // rows)))
            mine = move(jnp.where(upper_half == turn, stay, cross), pairs)
            other = move(mine, swap_rows(2))
            pair = jnp.where(is_own, turn, 1 - turn)
            parts += [mine, other, move(mine, swap_rows(1)), move(other, swap_rows(1))]
            for side in (odd, 1 - odd):
                places += [2 * (2 * pair + side) + plane, 2 * (2 * (1 - pair) + side) + 1 - plane]
        return parts, places

    def gather_whole(masked, row_index, col_index, panel, keep_of):
        row_block = lax.all_gather(masked, "col", axis=0, tiled=True)
        span = masked.shape[0] * rows
        own = lax.dynamic_slice_in_dim(row_block, lax.rem(col_index, ratio) * span, span, 0)
        own = jnp.where(row_index == col_index // ratio, own, jnp.zeros_like(own))
        block = lax.psum(own, "row")
        pieces = [block[i * masked.shape[0] : (i + 1) * masked.shape[0]] for i in range(rows)]
        return pieces, [jnp.int32(i) for i in range(rows)]

    gather = gather_pieces if rows == 4 else gather_whole

    def total_update(update, row_index):
        shape = update.shape
        flat = update.reshape(2, -1, shape[-1])
        odd = lax.rem(row_index, 2)
        keep = lax.dynamic_index_in_dim(flat, odd, 0, keepdims=False)
        give = lax.dynamic_index_in_dim(flat, 1 - odd, 0, keepdims=False)
        keep = keep + move(give, swap_rows(1))
        keep = keep + move(keep, swap_low())
        bit = 2
        while bit < rows:
            keep = keep + move(keep, swap_rows(bit))
            bit *= 2
        bit = 1
        while bit < line:
            keep = keep + move(keep, swap_line(bit))
            bit *= 2
        other = move(keep, swap_rows(1))
        even_part = jnp.where(odd == 0, keep, other)
        odd_part = jnp.where(odd == 0, other, keep)
        return jnp.stack([even_part, odd_part]).reshape(shape)

    def local(ancestor_inverse, panel, structure, diag_inverse):
        snodes, width = diag_inverse.shape[:2]
        depth = panel.shape[0]
        tile = min(512, depth)
        row_index, col_index = lax.axis_index("row"), lax.axis_index("col")
        low, place = lax.rem(col_index, 2), col_index // 2

        def keep_of(begin, length):
            same = math.gcd(length, width)
            blocks = length // same
            owners = (begin + jnp.arange(blocks, dtype=jnp.int32) * same) // width
            keep = jnp.take(structure, owners, axis=1).astype(BF16)
            keep = jnp.broadcast_to(keep.T[:, None, :, None], (blocks, same, snodes, width))
            return keep.reshape(length, snodes * width)

        keep = keep_of((row_index * cols + col_index) * depth, depth)
        masked = panel * keep
        order = jnp.asarray(table, jnp.int32)[place]
        cuts = [slice(k * width, (k + 1) * width) for k in range(snodes)]
        pieces, places = gather(masked, row_index, col_index, panel, keep_of)
        own = [[None] * line for _ in cuts]
        got = [[None] * line for _ in cuts]
        moved = [[] for _ in cuts]
        last = order

        def multiply(q):
            nonlocal last
            info = jnp.stack([order[q] * 2 + 1 - low, order[q] * 2 + low] + places)
            msgs, kept = product(info, ancestor_inverse, pieces, depth, tile, snodes)
            for k in range(snodes):
                own[k][q] = kept[k]
                got[k][q] = move(msgs[k], swap_low())
            last = msgs[-1]

        def advance(turn, k):
            slots, before, use = needs(turn)
            use = jnp.asarray(use, jnp.int32)[place]
            sent = pass_on(use, [(own[k][q], got[k][q]) for q in slots], [moved[k][t] for t in before])
            moved[k].append(move(sent, along(rounds[turn])))

        multiply(0)
        ready = 1
        for turn in range(len(rounds)):
            while ready < line and ready <= max(needs(turn)[0]) + (turn != 1):
                multiply(ready)
                ready += 1
            for k in range(snodes):
                advance(turn, k)
        while ready < line:
            multiply(ready)
            ready += 1
        _, before, use = needs(len(rounds))
        use = jnp.asarray(use, jnp.int32)[place]
        uppers, updates = [], []
        for k, cut in enumerate(cuts):
            arrived = [moved[k][t] for t in before]
            upper, update = finish(
                use, own[k][-1], got[k][-1], arrived, masked[:, cut], keep[:, cut], width
            )
            uppers.append(upper)
            updates.append(total_update(update, row_index))
        return jnp.concatenate(uppers, axis=1), diag_inverse - jnp.concatenate(updates)

    return local


def solution(mesh):
    return jax.shard_map(
        make_local(mesh.shape["row"], mesh.shape["col"]),
        mesh=mesh,
        in_specs=(P("row", "col"), P(("row", "col"), None), P(), P()),
        out_specs=(P(("row", "col"), None), P()),
        check_vma=False,
    )
```
